32 devices in a mesh: groups: 2 (over y), fib: 4 (over z), col: 4 (over x, core).
Axes of the slice: x: 2, y: 2, z: 4, core: 2. Of those that a mesh axis runs over, the one named last changes fastest.
Arguments:
- data_slab: float32 [256, 256, 2048], P(('groups', 'fib'), 'col'), parts along dimension 0, may hold values from -6 to 6
- first_factor: float32 [128, 96], replicated, may hold values from -0.5 to 0.5
- second_factor: float32 [256, 96], replicated, may hold values from -0.375 to 0.375
Outputs:
- core_slab: float32 [192, 96, 2048], P(('groups', 'col'), None, 'fib'), parts along dimension 0
The draws below stay inside these ranges and needn't reach their ends.
There are 2 independent parts, one for each index of `groups`. The reference program is written for one: setup_inputs(seed, part) draws one part's arguments, and reference() takes and returns one part's arrays. A program takes and returns all parts, laid end to end along the dimension named above; an argument that names none is the same for every part. Nothing has to cross between parts.
All inputs are finite; a program needn't handle non-finite values.
Results may differ from the reference program's by a relative error of at most 0.00007.
Values sent between devices are 32-bit elements; how exact they have to be, the bound alone decides.
A program may use at most 256 MiB of HBM per device.

```python
import jax
import jax.numpy as jnp
from jax import lax

I1 = 128
I2 = 256
R1 = 96
R2 = 96
CELLS = 2048


def with_spikes(drawn, own_key, source, target, blocks, factor):
    owner, partner = [(jnp.arange(drawn.shape[axis_at]) // (drawn.shape[axis_at] // blocks)).reshape([-1 if axis == axis_at else 1 for axis in range(drawn.ndim)]) for axis_at in (source, target)]
    chosen = jax.random.permutation(own_key, blocks)[partner]
    strong = (owner == chosen) | (owner == (partner + blocks // 2) % blocks)
    return jnp.where(strong, factor * drawn, drawn)


def steps_of(key, shape, cuts, low, top_value):
    def one(axis_at, shards_of):
        draws = jax.random.uniform(jax.random.fold_in(jax.random.fold_in(key, 6), axis_at), (shards_of,), jnp.float32, low / len(cuts), top_value / len(cuts))
        return jnp.repeat(jnp.exp(draws), shape[axis_at] // shards_of).reshape((-1,) + (1,) * (len(shape) - axis_at - 1))

    gain = one(*cuts[0])
    for cut in cuts[1:]:
        gain = gain * one(*cut)
    return gain


def normal_values(stream_key, extent, deviation, limit, shards=(), held_as=jnp.bfloat16):
    level = steps_of(stream_key, extent, shards, -0.22, 0.18) if shards else 1.0
    values = jax.random.normal(stream_key, extent, jnp.float32) * deviation * level
    return jnp.minimum(jnp.maximum(values, -limit), limit).astype(held_as)


def heavy_noise(own_key, dims, scale, limit, pieces, heavy, dtype=jnp.bfloat16):
    array = scale * jax.random.normal(own_key, dims, jnp.float32)
    if pieces:
        array = array * steps_of(own_key, dims, pieces, -0.22, 0.18)
    return jnp.clip(with_spikes(array, jax.random.fold_in(own_key, 3), *heavy), -limit, limit).astype(dtype)


def setup_inputs(seed: int = 0, part: int = 0) -> dict:
    keys = jax.random.split(jax.random.key(seed), 4)
    own_keys = jax.random.split(jax.random.fold_in(keys[3], part), 4)
    data_slab = heavy_noise(own_keys[0], (I1, I2, CELLS), 1.0, 6.0, ((0, 4), (1, 4)), (0, 2, 4, 2.0), jnp.float32)
    first_factor = normal_values(keys[1], (I1, R1), I1 ** -0.5, 0.5, (), jnp.float32)
    second_factor = normal_values(keys[2], (I2, R2), I2 ** -0.5, 0.375, (), jnp.float32)
    return {"data_slab": data_slab, "first_factor": first_factor, "second_factor": second_factor}


def reference(data_slab, first_factor, second_factor):
    first_core = jnp.einsum("ir,ijc->rjc", first_factor, data_slab, precision=lax.Precision.HIGHEST)
    core_slab = jnp.einsum("jq,rjc->rqc", second_factor, first_core, precision=lax.Precision.HIGHEST)
    return core_slab
```

```python
import functools

import jax
import jax.numpy as jnp
from jax import lax
from jax.experimental import pallas as pl
from jax.experimental.pallas import tpu as pltpu
from jax.sharding import PartitionSpec as P

MESH = pl.DeviceIdType.MESH
LANES = 128
Q_CHUNKS = 3
I_CHUNKS = 8
LAG = 2
OUT_LAG = 2


def second_mode(first_core, second_factor):
    return jnp.einsum(
        "jq,rjc->rqc",
        second_factor,
        lax.all_to_all(first_core, "col", split_axis=0, concat_axis=1, tiled=True),
        precision=lax.Precision.HIGHEST,
    )


def on_device(data_slab, first_factor, second_factor):
    moved_slab = lax.all_to_all(data_slab, "fib", split_axis=2, concat_axis=0, tiled=True)
    first_core = jnp.einsum(
        "ir,ijc->rjc", first_factor, moved_slab, precision=lax.Precision.HIGHEST
    )
    return second_mode(first_core, second_factor)


def split(values):
    high = values.astype(jnp.bfloat16)
    low = (values - high.astype(jnp.float32)).astype(jnp.bfloat16)
    return high, low


def kernel(
    nz, nq, ni, slab, f1, f2, out, xcat, pb, xr, g, rr, a1, a2,
    core_send, core_recv, core_local, x_send, x_recv, z_send, z_recv, o_send, o_recv, o_local,
):
    rows, jl, _ = slab.shape
    ic_rows = rows // ni
    qc_rows = pb.shape[4]
    ranks = f1.shape[1]
    own_ranks = out.shape[0]
    z = lax.axis_index("fib")
    k = lax.axis_index("col")
    x, core = k // 2, lax.rem(k, 2)
    sibling = 2 * x + (1 - core)
    partner = 2 * (1 - x) + core

    barrier = pltpu.get_barrier_semaphore()
    for e in range(1, 4):
        pl.semaphore_signal(
            barrier, inc=1, device_id={"col": lax.rem(k + e, 4)}, device_id_type=MESH
        )
    for d in range(1, nz):
        pl.semaphore_signal(
            barrier, inc=1, device_id={"fib": lax.rem(z + d, nz)}, device_id_type=MESH
        )
    pl.semaphore_wait(barrier, 3 + nz - 1)

    def wait(ref, sem):
        pltpu.make_async_copy(ref, ref, sem).wait()

    my_j = pl.ds(pl.multiple_of(core * jl, jl), jl)
    their_j = pl.ds(pl.multiple_of((1 - core) * jl, jl), jl)

    @pl.loop(0, ni)
    def _(ic):
        chunk = pl.ds(ic * ic_rows, ic_rows)
        for zi in range(nz):
            base = zi * 4 * LANES
            cells = pl.ds(zi * 2 * LANES, 2 * LANES)
            theirs = pl.ds(pl.multiple_of(base + (1 - core) * 2 * LANES, 2 * LANES), 2 * LANES)
            mine = pl.ds(pl.multiple_of(base + core * 2 * LANES, 2 * LANES), 2 * LANES)
            pltpu.make_async_remote_copy(
                src_ref=slab.at[chunk, :, theirs],
                dst_ref=xcat.at[chunk, my_j, cells],
                send_sem=core_send.at[ic],
                recv_sem=core_recv.at[ic],
                device_id={"col": sibling},
                device_id_type=MESH,
            ).start()
            pltpu.make_async_copy(
                slab.at[chunk, :, mine], xcat.at[chunk, my_j, cells], core_local.at[ic]
            ).start()

    def place(ref, factor, size):
        high, low = split(factor)
        depth = factor.shape[1]
        for qc in range(ref.shape[0]):
            at = slice(qc * size, (qc + 1) * size)
            ref[qc, :size, :depth] = high[at]
            ref[qc, :size, depth:] = high[at]
            ref[qc, size:, :depth] = low[at]
            ref[qc, size:, depth:] = jnp.zeros_like(low[at])

    place(a2, f2[pl.ds(pl.multiple_of(x * 2 * jl, 2 * jl), 2 * jl), :].T, qc_rows)
    place(a1, f1[...].T, ranks)

    def product(factor, values):
        high, low = split(values)
        both = jnp.dot(
            factor, jnp.concatenate([high, low], axis=0), preferred_element_type=jnp.float32
        )
        half = both.shape[0] // 2
        return both[:half] + both[half:]

    def to_second_rank(s):
        qc, ic = s // ni, lax.rem(s, ni)
        chunk = pl.ds(ic * ic_rows, ic_rows)

        @pl.when(qc == 0)
        def _():
            wait(xcat.at[chunk, my_j], core_local.at[ic])
            wait(xcat.at[chunk, their_j], core_recv.at[ic])

        @pl.loop(0, ic_rows)
        def _(step):
            i = ic * ic_rows + step
            for zi in range(nz):
                part = product(a2[qc], xcat[i, :, zi * 2 * LANES : (zi + 1) * 2 * LANES])
                pb[0, qc, zi, i] = part[:, :LANES]
                pb[1, qc, zi, i] = part[:, LANES:]

        pltpu.make_async_remote_copy(
            src_ref=pb.at[1 - x, qc, :, chunk],
            dst_ref=xr.at[qc, :, chunk],
            send_sem=x_send.at[s],
            recv_sem=x_recv.at[s],
            device_id={"col": partner},
            device_id_type=MESH,
        ).start()

    def add_and_send(s):
        qc, ic = s // ni, lax.rem(s, ni)
        chunk = pl.ds(ic * ic_rows, ic_rows)
        wait(xr.at[qc, :, chunk], x_recv.at[s])
        for zi in range(nz):
            pb[x, qc, zi, chunk] = pb[x, qc, zi, chunk] + xr[qc, zi, chunk]
        g[qc, z, chunk] = pb[x, qc, z, chunk]
        for d in range(1, nz):
            peer = lax.rem(z + d, nz)
            pltpu.make_async_remote_copy(
                src_ref=pb.at[x, qc, peer, chunk],
                dst_ref=g.at[qc, z, chunk],
                send_sem=z_send.at[qc, d - 1],
                recv_sem=z_recv.at[qc, d - 1],
                device_id={"fib": peer},
                device_id_type=MESH,
            ).start()

    def sub(column):
        start = (lax.rem(column, 2) * 2 + column // 2) * LANES
        return pl.ds(pl.multiple_of(start, LANES), LANES)

    def to_first_rank(qc):
        for d in range(1, nz):
            wait(g.at[qc, lax.rem(z - d + nz, nz)], z_recv.at[qc, d - 1])
        points = nz * rows
        flat = g.at[qc].reshape(points * qc_rows, LANES)
        ranked = rr.at[qc].reshape(ranks * qc_rows, LANES)

        @pl.loop(0, qc_rows // 2)
        def _(pair):
            q = 2 * pair
            values = jnp.concatenate(
                [flat[pl.ds(q + t, points, stride=qc_rows), :] for t in range(2)], axis=1
            )
            part = product(a1[0], values)
            for t in range(2):
                ranked[pl.ds(q + t, ranks, stride=qc_rows), :] = part[
                    :, t * LANES : (t + 1) * LANES
                ]

        qs = pl.ds(pl.multiple_of(qc * qc_rows, qc_rows), qc_rows)
        for e in range(1, 4):
            peer = lax.rem(k + e, 4)
            pltpu.make_async_remote_copy(
                src_ref=rr.at[qc, pl.ds(peer * own_ranks, own_ranks)],
                dst_ref=out.at[:, qs, sub(k)],
                send_sem=o_send.at[qc, e - 1],
                recv_sem=o_recv.at[qc, e - 1],
                device_id={"col": peer},
                device_id_type=MESH,
            ).start()
        pltpu.make_async_copy(
            rr.at[qc, pl.ds(k * own_ranks, own_ranks)], out.at[:, qs, sub(k)], o_local.at[qc]
        ).start()

    steps = nq * ni

    @pl.loop(0, steps + LAG + OUT_LAG)
    def _(s):
        @pl.when(s < steps)
        def _():
            to_second_rank(s)

        @pl.when((s >= LAG) & (s < steps + LAG))
        def _():
            add_and_send(s - LAG)

        done = s - (LAG + OUT_LAG) + 1

        @pl.when((done > 0) & (lax.rem(done, ni) == 0))
        def _():
            to_first_rank(done // ni - 1)

    @pl.loop(0, ni)
    def _(ic):
        chunk = pl.ds(ic * ic_rows, ic_rows)
        wait(xcat.at[chunk, my_j], core_send.at[ic])

    @pl.loop(0, steps)
    def _(s):
        qc, ic = s // ni, lax.rem(s, ni)
        wait(pb.at[1 - x, qc, :, pl.ds(ic * ic_rows, ic_rows)], x_send.at[s])

    for qc in range(nq):
        qs = pl.ds(qc * qc_rows, qc_rows)
        for d in range(1, nz):
            wait(pb.at[x, qc, lax.rem(z + d, nz)], z_send.at[qc, d - 1])
        for e in range(1, 4):
            wait(rr.at[qc, pl.ds(lax.rem(k + e, 4) * own_ranks, own_ranks)], o_send.at[qc, e - 1])
            wait(out.at[:, qs, sub(lax.rem(k - e + 4, 4))], o_recv.at[qc, e - 1])
        wait(out.at[:, qs, sub(k)], o_local.at[qc])


def fused(nz, data_slab, first_factor, second_factor):
    rows, jl, cells = data_slab.shape
    ranks, qs = first_factor.shape[1], second_factor.shape[1]
    nq, ni = Q_CHUNKS, I_CHUNKS
    qc_rows = qs // nq
    f32, bf16 = jnp.float32, jnp.bfloat16
    dma = pltpu.SemaphoreType.DMA
    scratch = [
        pltpu.VMEM((rows, 2 * jl, cells // 2), f32),
        pltpu.VMEM((2, nq, nz, rows, qc_rows, LANES), f32),
        pltpu.VMEM((nq, nz, rows, qc_rows, LANES), f32),
        pltpu.VMEM((nq, nz, rows, qc_rows, LANES), f32),
        pltpu.VMEM((nq, ranks, qc_rows, LANES), f32),
        pltpu.VMEM((1, 2 * ranks, 2 * nz * rows), bf16),
        pltpu.VMEM((nq, 2 * qc_rows, 4 * jl), bf16),
        dma((ni,)), dma((ni,)), dma((ni,)),
        dma((nq * ni,)), dma((nq * ni,)),
        dma((nq, nz - 1)), dma((nq, nz - 1)),
        dma((nq, 3)), dma((nq, 3)), dma((nq,)),
    ]
    return pl.pallas_call(
        functools.partial(kernel, nz, nq, ni),
        out_shape=jax.ShapeDtypeStruct((ranks // 4, qs, cells // nz), f32),
        in_specs=[
            pl.BlockSpec(memory_space=pl.ANY),
            pl.BlockSpec(memory_space=pltpu.VMEM),
            pl.BlockSpec(memory_space=pltpu.VMEM),
        ],
        out_specs=pl.BlockSpec(memory_space=pl.ANY),
        scratch_shapes=scratch,
        compiler_params=pltpu.CompilerParams(
            collective_id=0, has_side_effects=True, vmem_limit_bytes=56 * 1024 * 1024
        ),
    )(data_slab, first_factor, second_factor)


def solution(mesh):
    nz, nc = mesh.shape["fib"], mesh.shape["col"]

    def on_each(data_slab, first_factor, second_factor):
        cells = data_slab.shape[2]
        if nc == 4 and nz > 1 and cells == nz * nc * LANES:
            return fused(nz, data_slab, first_factor, second_factor)
        return on_device(data_slab, first_factor, second_factor)

    in_specs = (P(("groups", "fib"), "col", None), P(), P())
    out_specs = P(("groups", "col"), None, "fib")
    return jax.shard_map(
        on_each, mesh=mesh, in_specs=in_specs, out_specs=out_specs, check_vma=False
    )
```

```python
import functools

import jax
import jax.numpy as jnp
from jax import lax
from jax.experimental import pallas as pl
from jax.experimental.pallas import tpu as pltpu
from jax.sharding import PartitionSpec as P

MESH = pl.DeviceIdType.MESH
LANES = 128
Q_CHUNKS = 6
I_CHUNKS = 4
LAG = 2
VMEM_MIB = 50


def second_mode(first_core, second_factor):
    return jnp.einsum(
        "jq,rjc->rqc",
        second_factor,
        lax.all_to_all(first_core, "col", split_axis=0, concat_axis=1, tiled=True),
        precision=lax.Precision.HIGHEST,
    )


def on_device(data_slab, first_factor, second_factor):
    moved_slab = lax.all_to_all(data_slab, "fib", split_axis=2, concat_axis=0, tiled=True)
    first_core = jnp.einsum(
        "ir,ijc->rjc", first_factor, moved_slab, precision=lax.Precision.HIGHEST
    )
    return second_mode(first_core, second_factor)


def split(values):
    high = values.astype(jnp.bfloat16)
    low = (values - high.astype(jnp.float32)).astype(jnp.bfloat16)
    return high, low


def kernel(
    nz, nq, ni, slab, f1, f2, out, xcat, pb, xr, g, gf, rr, rf, rx, a1, a2,
    core_send, core_recv, core_local, x_send, x_recv, z_send, z_recv, zf_send, zf_recv,
    o_send, o_recv, o_local, f_send, f_recv, s_send, s_recv, s_local,
):
    rows, jl, _ = slab.shape
    ic_rows = rows // ni
    qc_rows = pb.shape[4]
    ranks = f1.shape[0]
    own_ranks = out.shape[0]
    points = nz * rows
    last = nq - 1
    z = lax.axis_index("fib")
    k = lax.axis_index("col")
    x, core = k // 2, lax.rem(k, 2)
    sibling = 2 * x + (1 - core)
    partner = 2 * (1 - x) + core

    barrier = pltpu.get_barrier_semaphore()
    for e in range(1, 4):
        pl.semaphore_signal(
            barrier, inc=1, device_id={"col": lax.rem(k + e, 4)}, device_id_type=MESH
        )
    for d in range(1, nz):
        pl.semaphore_signal(
            barrier, inc=1, device_id={"fib": lax.rem(z + d, nz)}, device_id_type=MESH
        )
    pl.semaphore_wait(barrier, 3 + nz - 1)

    def wait(ref, sem):
        pltpu.make_async_copy(ref, ref, sem).wait()

    def send(src, dst, send_sem, recv_sem, target):
        pltpu.make_async_remote_copy(
            src_ref=src,
            dst_ref=dst,
            send_sem=send_sem,
            recv_sem=recv_sem,
            device_id=target,
            device_id_type=MESH,
        ).start()

    def rows_of(start, size):
        return pl.ds(pl.multiple_of(start, size), size)

    my_j, their_j = rows_of(core * jl, jl), rows_of((1 - core) * jl, jl)

    @pl.loop(0, ni)
    def _(ic):
        chunk = pl.ds(ic * ic_rows, ic_rows)
        for zi in range(nz):
            base = zi * 4 * LANES
            cells = pl.ds(zi * 2 * LANES, 2 * LANES)
            theirs = rows_of(base + (1 - core) * 2 * LANES, 2 * LANES)
            mine = rows_of(base + core * 2 * LANES, 2 * LANES)
            send(
                slab.at[chunk, :, theirs], xcat.at[chunk, my_j, cells],
                core_send.at[ic], core_recv.at[ic], {"col": sibling},
            )
            pltpu.make_async_copy(
                slab.at[chunk, :, mine], xcat.at[chunk, my_j, cells], core_local.at[ic]
            ).start()

    def place(ref, factor):
        high, low = split(factor)
        size, depth = factor.shape
        ref[:size, :depth] = high
        ref[:size, depth:] = high
        ref[size:, :depth] = low
        ref[size:, depth:] = jnp.zeros_like(low)

    place(a2, f2[:, rows_of(x * 2 * jl, 2 * jl)])
    place(a1, f1[...])

    def product(factor, values):
        high, low = split(values)
        both = jnp.dot(
            factor, jnp.concatenate([high, low], axis=0), preferred_element_type=jnp.float32
        )
        half = both.shape[0] // 2
        return both[:half] + both[half:]

    def to_second_rank(ic):
        chunk = pl.ds(ic * ic_rows, ic_rows)
        wait(xcat.at[chunk, my_j], core_local.at[ic])
        wait(xcat.at[chunk, their_j], core_recv.at[ic])

        @pl.loop(0, ic_rows)
        def _(step):
            i = ic * ic_rows + step
            for zi in range(nz):
                part = product(a2[...], xcat[i, :, zi * 2 * LANES : (zi + 1) * 2 * LANES])
                for qc in range(nq):
                    at = slice(qc * qc_rows, (qc + 1) * qc_rows)
                    pb[0, qc, zi, i] = part[at, :LANES]
                    pb[1, qc, zi, i] = part[at, LANES:]

    def send_last(ic):
        chunk = pl.ds(ic * ic_rows, ic_rows)
        for d in range(1, nz):
            peer = lax.rem(z + d, nz)
            send(
                pb.at[:, last, peer, chunk], gf.at[:, z, chunk],
                zf_send.at[d - 1], zf_recv.at[d - 1], {"fib": peer},
            )
        gf[:, z, chunk] = pb[:, last, z, chunk]

    def send_half(s):
        qc, ic = s // ni, lax.rem(s, ni)
        chunk = pl.ds(ic * ic_rows, ic_rows)
        send(
            pb.at[1 - x, qc, :, chunk], xr.at[qc, :, chunk],
            x_send.at[s], x_recv.at[s], {"col": partner},
        )

    def add_and_send(s):
        qc, ic = s // ni, lax.rem(s, ni)
        chunk = pl.ds(ic * ic_rows, ic_rows)
        wait(xr.at[qc, :, chunk], x_recv.at[s])
        for zi in range(nz):
            pb[x, qc, zi, chunk] = pb[x, qc, zi, chunk] + xr[qc, zi, chunk]
        g[qc, z, chunk] = pb[x, qc, z, chunk]
        for d in range(1, nz):
            peer = lax.rem(z + d, nz)
            send(
                pb.at[x, qc, peer, chunk], g.at[qc, z, chunk],
                z_send.at[qc, d - 1], z_recv.at[qc, d - 1], {"fib": peer},
            )

    def sub(column):
        return rows_of((lax.rem(column, 2) * 2 + column // 2) * LANES, LANES)

    def to_first_rank(qc):
        for d in range(1, nz):
            wait(g.at[qc, lax.rem(z - d + nz, nz)], z_recv.at[qc, d - 1])
        flat = g.at[qc].reshape(points * qc_rows, LANES)
        ranked = rr.at[qc].reshape(ranks * qc_rows, LANES)

        @pl.loop(0, qc_rows // 2)
        def _(pair):
            q = 2 * pair
            values = jnp.concatenate(
                [flat[pl.ds(q + t, points, stride=qc_rows), :] for t in range(2)], axis=1
            )
            part = product(a1[...], values)
            for t in range(2):
                ranked[pl.ds(q + t, ranks, stride=qc_rows), :] = part[
                    :, t * LANES : (t + 1) * LANES
                ]

        qs = rows_of(qc * qc_rows, qc_rows)
        for e in range(1, 4):
            peer = lax.rem(k + e, 4)
            send(
                rr.at[qc, pl.ds(peer * own_ranks, own_ranks)], out.at[:, qs, sub(k)],
                o_send.at[qc, e - 1], o_recv.at[qc, e - 1], {"col": peer},
            )
        pltpu.make_async_copy(
            rr.at[qc, pl.ds(k * own_ranks, own_ranks)], out.at[:, qs, sub(k)], o_local.at[qc]
        ).start()

    half = 2 * own_ranks
    my_half, their_half = pl.ds(x * half, half), pl.ds((1 - x) * half, half)
    last_qs = pl.ds(last * qc_rows, qc_rows)

    def last_to_first_rank():
        for d in range(1, nz):
            wait(gf.at[:, lax.rem(z - d + nz, nz)], zf_recv.at[d - 1])
        flats = [gf.at[t].reshape(points * qc_rows, LANES) for t in range(2)]
        ranked = [rf.at[t].reshape(ranks * qc_rows, LANES) for t in range(2)]

        @pl.loop(0, qc_rows)
        def _(q):
            values = jnp.concatenate(
                [flat[pl.ds(q, points, stride=qc_rows), :] for flat in flats], axis=1
            )
            part = product(a1[...], values)
            for t in range(2):
                ranked[t][pl.ds(q, ranks, stride=qc_rows), :] = part[
                    :, t * LANES : (t + 1) * LANES
                ]

        send(rf.at[:, their_half], rx, f_send, f_recv, {"col": partner})

    def last_cells(which, t):
        return rows_of((which * 2 + t) * LANES, LANES)

    def last_out():
        wait(rx, f_recv)
        for t in range(2):
            rx[t] = rx[t] + rf[t, my_half]
            place_at = out.at[:, last_qs, last_cells(core, t)]
            send(
                rx.at[t, pl.ds((1 - core) * own_ranks, own_ranks)], place_at,
                s_send.at[t], s_recv.at[t], {"col": sibling},
            )
            pltpu.make_async_copy(
                rx.at[t, pl.ds(core * own_ranks, own_ranks)], place_at, s_local.at[t]
            ).start()

    steps = last * ni

    @pl.loop(0, steps + LAG)
    def _(s):
        @pl.when(s < ni)
        def _():
            to_second_rank(s)

        @pl.when(s < steps)
        def _():
            send_half(s)

        @pl.when(s < ni)
        def _():
            send_last(s)

        @pl.when(s >= LAG)
        def _():
            add_and_send(s - LAG)

    for qc in range(last):
        to_first_rank(qc)
        if qc == 0:
            last_to_first_rank()
        if qc == 1:
            last_out()

    @pl.loop(0, ni)
    def _(ic):
        chunk = pl.ds(ic * ic_rows, ic_rows)
        wait(xcat.at[chunk, my_j], core_send.at[ic])

    @pl.loop(0, steps)
    def _(s):
        qc, ic = s // ni, lax.rem(s, ni)
        wait(pb.at[1 - x, qc, :, pl.ds(ic * ic_rows, ic_rows)], x_send.at[s])

    for d in range(1, nz):
        wait(pb.at[:, last, lax.rem(z + d, nz)], zf_send.at[d - 1])
    wait(rf.at[:, their_half], f_send)
    for t in range(2):
        wait(rx.at[t, pl.ds((1 - core) * own_ranks, own_ranks)], s_send.at[t])
        wait(out.at[:, last_qs, last_cells(1 - core, t)], s_recv.at[t])
        wait(out.at[:, last_qs, last_cells(core, t)], s_local.at[t])
    for qc in range(last):
        qs = pl.ds(qc * qc_rows, qc_rows)
        for d in range(1, nz):
            wait(pb.at[x, qc, lax.rem(z + d, nz)], z_send.at[qc, d - 1])
        for e in range(1, 4):
            wait(rr.at[qc, pl.ds(lax.rem(k + e, 4) * own_ranks, own_ranks)], o_send.at[qc, e - 1])
            wait(out.at[:, qs, sub(lax.rem(k - e + 4, 4))], o_recv.at[qc, e - 1])
        wait(out.at[:, qs, sub(k)], o_local.at[qc])


def fused(nz, data_slab, first_factor, second_factor):
    rows, jl, cells = data_slab.shape
    ranks, qs = first_factor.shape[1], second_factor.shape[1]
    nq, ni = Q_CHUNKS, I_CHUNKS
    qc_rows = qs // nq
    f32, bf16 = jnp.float32, jnp.bfloat16
    dma = pltpu.SemaphoreType.DMA
    last = nq - 1
    scratch = [
        pltpu.VMEM((rows, 2 * jl, cells // 2), f32),
        pltpu.VMEM((2, nq, nz, rows, qc_rows, LANES), f32),
        pltpu.VMEM((last, nz, rows, qc_rows, LANES), f32),
        pltpu.VMEM((last, nz, rows, qc_rows, LANES), f32),
        pltpu.VMEM((2, nz, rows, qc_rows, LANES), f32),
        pltpu.VMEM((last, ranks, qc_rows, LANES), f32),
        pltpu.VMEM((2, ranks, qc_rows, LANES), f32),
        pltpu.VMEM((2, ranks // 2, qc_rows, LANES), f32),
        pltpu.VMEM((2 * ranks, 2 * nz * rows), bf16),
        pltpu.VMEM((2 * qs, 4 * jl), bf16),
        dma((ni,)), dma((ni,)), dma((ni,)),
        dma((last * ni,)), dma((last * ni,)),
        dma((last, nz - 1)), dma((last, nz - 1)),
        dma((nz - 1,)), dma((nz - 1,)),
        dma((last, 3)), dma((last, 3)), dma((last,)),
        dma, dma,
        dma((2,)), dma((2,)), dma((2,)),
    ]
    return pl.pallas_call(
        functools.partial(kernel, nz, nq, ni),
        out_shape=jax.ShapeDtypeStruct((ranks // 4, qs, cells // nz), f32),
        in_specs=[
            pl.BlockSpec(memory_space=pl.ANY),
            pl.BlockSpec(memory_space=pltpu.VMEM),
            pl.BlockSpec(memory_space=pltpu.VMEM),
        ],
        out_specs=pl.BlockSpec(memory_space=pl.ANY),
        scratch_shapes=scratch,
        compiler_params=pltpu.CompilerParams(
            collective_id=0, has_side_effects=True, vmem_limit_bytes=VMEM_MIB * 1024 * 1024
        ),
    )(data_slab, first_factor.T, second_factor.T)


def solution(mesh):
    nz, nc = mesh.shape["fib"], mesh.shape["col"]

    def on_each(data_slab, first_factor, second_factor):
        cells = data_slab.shape[2]
        if nc == 4 and nz > 1 and cells == nz * nc * LANES:
            return fused(nz, data_slab, first_factor, second_factor)
        return on_device(data_slab, first_factor, second_factor)

    in_specs = (P(("groups", "fib"), "col", None), P(), P())
    out_specs = P(("groups", "col"), None, "fib")
    return jax.shard_map(
        on_each, mesh=mesh, in_specs=in_specs, out_specs=out_specs, check_vma=False
    )
```

```python
import functools

import jax
import jax.numpy as jnp
from jax import lax
from jax.experimental import pallas as pl
from jax.experimental.pallas import tpu as pltpu
from jax.sharding import PartitionSpec as P

MESH = pl.DeviceIdType.MESH
LANES = 128
Q_CHUNKS = 6
I_CHUNKS = 8
LAG = 4
F_AT = 1
OUT_AT = 2
ORDER = (2, 3, 1)
VMEM_MIB = 48


def second_mode(first_core, second_factor):
    return jnp.einsum(
        "jq,rjc->rqc",
        second_factor,
        lax.all_to_all(first_core, "col", split_axis=0, concat_axis=1, tiled=True),
        precision=lax.Precision.HIGHEST,
    )


def on_device(data_slab, first_factor, second_factor):
    moved_slab = lax.all_to_all(data_slab, "fib", split_axis=2, concat_axis=0, tiled=True)
    first_core = jnp.einsum(
        "ir,ijc->rjc", first_factor, moved_slab, precision=lax.Precision.HIGHEST
    )
    return second_mode(first_core, second_factor)


def swapped(z, d):
    return {1: z + 1 - 2 * lax.rem(z, 2), 2: lax.rem(z + 2, 4), 3: 3 - z}[d]


def split(values):
    high = values.astype(jnp.bfloat16)
    low = (values - high.astype(jnp.float32)).astype(jnp.bfloat16)
    return high, low


def kernel(
    nz, nq, ni, slab, f1, f2, out, xcat, pb, xr, g, gf, rr, rf, rx, a1, a2,
    core_send, core_recv, core_local, x_send, x_recv, z_send, z_recv, zf_send, zf_recv,
    o_send, o_recv, o_local, f_send, f_recv, s_send, s_recv, s_local,
):
    rows, jl, _ = slab.shape
    ic_rows = rows // ni
    qc_rows = pb.shape[4]
    ranks = f1.shape[0]
    own_ranks = out.shape[0]
    points = nz * rows
    last = nq - 1
    z = lax.axis_index("fib")
    k = lax.axis_index("col")
    x, core = k // 2, lax.rem(k, 2)
    sibling = 2 * x + (1 - core)
    partner = 2 * (1 - x) + core

    barrier = pltpu.get_barrier_semaphore()
    for e in range(1, 4):
        pl.semaphore_signal(
            barrier, inc=1, device_id={"col": lax.rem(k + e, 4)}, device_id_type=MESH
        )
    for d in range(1, nz):
        pl.semaphore_signal(
            barrier, inc=1, device_id={"fib": swapped(z, d)}, device_id_type=MESH
        )
    pl.semaphore_wait(barrier, 3 + nz - 1)

    def wait(ref, sem):
        pltpu.make_async_copy(ref, ref, sem).wait()

    def send(src, dst, send_sem, recv_sem, target):
        pltpu.make_async_remote_copy(
            src_ref=src,
            dst_ref=dst,
            send_sem=send_sem,
            recv_sem=recv_sem,
            device_id=target,
            device_id_type=MESH,
        ).start()

    def rows_of(start, size):
        return pl.ds(pl.multiple_of(start, size), size)

    my_j, their_j = rows_of(core * jl, jl), rows_of((1 - core) * jl, jl)

    @pl.loop(0, ni)
    def _(ic):
        chunk = pl.ds(ic * ic_rows, ic_rows)
        for zi in range(nz):
            base = zi * 4 * LANES
            cells = pl.ds(zi * 2 * LANES, 2 * LANES)
            theirs = rows_of(base + (1 - core) * 2 * LANES, 2 * LANES)
            mine = rows_of(base + core * 2 * LANES, 2 * LANES)
            send(
                slab.at[chunk, :, theirs], xcat.at[chunk, my_j, cells],
                core_send.at[ic], core_recv.at[ic], {"col": sibling},
            )
            pltpu.make_async_copy(
                slab.at[chunk, :, mine], xcat.at[chunk, my_j, cells], core_local.at[ic]
            ).start()

    def place(ref, factor):
        high, low = split(factor)
        size, depth = factor.shape
        ref[:size, :depth] = high
        ref[:size, depth:] = high
        ref[size:, :depth] = low
        ref[size:, depth:] = jnp.zeros_like(low)

    place(a2, f2[:, rows_of(x * 2 * jl, 2 * jl)])
    place(a1, f1[...])

    def product(factor, values):
        high, low = split(values)
        both = jnp.dot(
            factor, jnp.concatenate([high, low], axis=0), preferred_element_type=jnp.float32
        )
        half = both.shape[0] // 2
        return both[:half] + both[half:]

    def to_second_rank(ic):
        chunk = pl.ds(ic * ic_rows, ic_rows)
        wait(xcat.at[chunk, my_j], core_local.at[ic])
        wait(xcat.at[chunk, their_j], core_recv.at[ic])

        @pl.loop(0, ic_rows)
        def _(step):
            i = ic * ic_rows + step
            for zi in range(nz):
                part = product(a2[...], xcat[i, :, zi * 2 * LANES : (zi + 1) * 2 * LANES])
                for qc in range(nq):
                    at = slice(qc * qc_rows, (qc + 1) * qc_rows)
                    pb[0, qc, zi, i] = part[at, :LANES]
                    pb[1, qc, zi, i] = part[at, LANES:]

    def send_last(ic):
        chunk = pl.ds(ic * ic_rows, ic_rows)
        for d in ORDER:
            peer = swapped(z, d)
            send(
                pb.at[:, last, peer, chunk], gf.at[:, z, chunk],
                zf_send.at[d - 1], zf_recv.at[d - 1], {"fib": peer},
            )
        gf[:, z, chunk] = pb[:, last, z, chunk]

    def send_half(s):
        qc, ic = s // ni, lax.rem(s, ni)
        chunk = pl.ds(ic * ic_rows, ic_rows)
        send(
            pb.at[1 - x, qc, :, chunk], xr.at[qc, :, chunk],
            x_send.at[s], x_recv.at[s], {"col": partner},
        )

    def add_and_send(s):
        qc, ic = s // ni, lax.rem(s, ni)
        chunk = pl.ds(ic * ic_rows, ic_rows)
        wait(xr.at[qc, :, chunk], x_recv.at[s])
        for zi in range(nz):
            pb[x, qc, zi, chunk] = pb[x, qc, zi, chunk] + xr[qc, zi, chunk]
        g[qc, z, chunk] = pb[x, qc, z, chunk]
        for d in ORDER:
            peer = swapped(z, d)
            send(
                pb.at[x, qc, peer, chunk], g.at[qc, z, chunk],
                z_send.at[qc, d - 1], z_recv.at[qc, d - 1], {"fib": peer},
            )

    def sub(column):
        return rows_of((lax.rem(column, 2) * 2 + column // 2) * LANES, LANES)

    def to_first_rank(qc):
        for d in range(1, nz):
            wait(g.at[qc, swapped(z, d)], z_recv.at[qc, d - 1])
        flat = g.at[qc].reshape(points * qc_rows, LANES)
        ranked = rr.at[qc].reshape(ranks * qc_rows, LANES)

        @pl.loop(0, qc_rows // 2)
        def _(pair):
            q = 2 * pair
            values = jnp.concatenate(
                [flat[pl.ds(q + t, points, stride=qc_rows), :] for t in range(2)], axis=1
            )
            part = product(a1[...], values)
            for t in range(2):
                ranked[pl.ds(q + t, ranks, stride=qc_rows), :] = part[
                    :, t * LANES : (t + 1) * LANES
                ]

        qs = rows_of(qc * qc_rows, qc_rows)
        for e in range(1, 4):
            peer = lax.rem(k + e, 4)
            send(
                rr.at[qc, pl.ds(peer * own_ranks, own_ranks)], out.at[:, qs, sub(k)],
                o_send.at[qc, e - 1], o_recv.at[qc, e - 1], {"col": peer},
            )
        pltpu.make_async_copy(
            rr.at[qc, pl.ds(k * own_ranks, own_ranks)], out.at[:, qs, sub(k)], o_local.at[qc]
        ).start()

    half = 2 * own_ranks
    my_half, their_half = pl.ds(x * half, half), pl.ds((1 - x) * half, half)
    last_qs = pl.ds(last * qc_rows, qc_rows)

    def last_to_first_rank():
        for d in range(1, nz):
            wait(gf.at[:, swapped(z, d)], zf_recv.at[d - 1])
        flats = [gf.at[t].reshape(points * qc_rows, LANES) for t in range(2)]
        ranked = [rf.at[t].reshape(ranks * qc_rows, LANES) for t in range(2)]

        @pl.loop(0, qc_rows)
        def _(q):
            values = jnp.concatenate(
                [flat[pl.ds(q, points, stride=qc_rows), :] for flat in flats], axis=1
            )
            part = product(a1[...], values)
            for t in range(2):
                ranked[t][pl.ds(q, ranks, stride=qc_rows), :] = part[
                    :, t * LANES : (t + 1) * LANES
                ]

        send(rf.at[:, their_half], rx, f_send, f_recv, {"col": partner})

    def last_cells(which, t):
        return rows_of((which * 2 + t) * LANES, LANES)

    def last_out():
        wait(rx, f_recv)
        for t in range(2):
            rx[t] = rx[t] + rf[t, my_half]
            place_at = out.at[:, last_qs, last_cells(core, t)]
            send(
                rx.at[t, pl.ds((1 - core) * own_ranks, own_ranks)], place_at,
                s_send.at[t], s_recv.at[t], {"col": sibling},
            )
            pltpu.make_async_copy(
                rx.at[t, pl.ds(core * own_ranks, own_ranks)], place_at, s_local.at[t]
            ).start()

    steps = last * ni

    @pl.loop(0, steps + LAG)
    def _(s):
        @pl.when(s < ni)
        def _():
            to_second_rank(s)

        @pl.when(s < steps)
        def _():
            send_half(s)

        @pl.when(s < ni)
        def _():
            send_last(s)

        @pl.when(s >= LAG)
        def _():
            add_and_send(s - LAG)

    pl.loop(0, F_AT)(to_first_rank)
    last_to_first_rank()
    pl.loop(F_AT, OUT_AT)(to_first_rank)
    last_out()
    pl.loop(OUT_AT, last)(to_first_rank)

    @pl.loop(0, ni)
    def _(ic):
        chunk = pl.ds(ic * ic_rows, ic_rows)
        wait(xcat.at[chunk, my_j], core_send.at[ic])

    @pl.loop(0, steps)
    def _(s):
        qc, ic = s // ni, lax.rem(s, ni)
        wait(pb.at[1 - x, qc, :, pl.ds(ic * ic_rows, ic_rows)], x_send.at[s])

    for d in range(1, nz):
        wait(pb.at[:, last, swapped(z, d)], zf_send.at[d - 1])
    wait(rf.at[:, their_half], f_send)
    for t in range(2):
        wait(rx.at[t, pl.ds((1 - core) * own_ranks, own_ranks)], s_send.at[t])
        wait(out.at[:, last_qs, last_cells(1 - core, t)], s_recv.at[t])
        wait(out.at[:, last_qs, last_cells(core, t)], s_local.at[t])
    for qc in range(last):
        qs = pl.ds(qc * qc_rows, qc_rows)
        for d in range(1, nz):
            wait(pb.at[x, qc, swapped(z, d)], z_send.at[qc, d - 1])
        for e in range(1, 4):
            wait(rr.at[qc, pl.ds(lax.rem(k + e, 4) * own_ranks, own_ranks)], o_send.at[qc, e - 1])
            wait(out.at[:, qs, sub(lax.rem(k - e + 4, 4))], o_recv.at[qc, e - 1])
        wait(out.at[:, qs, sub(k)], o_local.at[qc])


def fused(nz, data_slab, first_factor, second_factor):
    rows, jl, cells = data_slab.shape
    ranks, qs = first_factor.shape[1], second_factor.shape[1]
    nq, ni = Q_CHUNKS, I_CHUNKS
    qc_rows = qs // nq
    f32, bf16 = jnp.float32, jnp.bfloat16
    dma = pltpu.SemaphoreType.DMA
    last = nq - 1
    scratch = [
        pltpu.VMEM((rows, 2 * jl, cells // 2), f32),
        pltpu.VMEM((2, nq, nz, rows, qc_rows, LANES), f32),
        pltpu.VMEM((last, nz, rows, qc_rows, LANES), f32),
        pltpu.VMEM((last, nz, rows, qc_rows, LANES), f32),
        pltpu.VMEM((2, nz, rows, qc_rows, LANES), f32),
        pltpu.VMEM((last, ranks, qc_rows, LANES), f32),
        pltpu.VMEM((2, ranks, qc_rows, LANES), f32),
        pltpu.VMEM((2, ranks // 2, qc_rows, LANES), f32),
        pltpu.VMEM((2 * ranks, 2 * nz * rows), bf16),
        pltpu.VMEM((2 * qs, 4 * jl), bf16),
        dma((ni,)), dma((ni,)), dma((ni,)),
        dma((last * ni,)), dma((last * ni,)),
        dma((last, nz - 1)), dma((last, nz - 1)),
        dma((nz - 1,)), dma((nz - 1,)),
        dma((last, 3)), dma((last, 3)), dma((last,)),
        dma, dma,
        dma((2,)), dma((2,)), dma((2,)),
    ]
    return pl.pallas_call(
        functools.partial(kernel, nz, nq, ni),
        out_shape=jax.ShapeDtypeStruct((ranks // 4, qs, cells // nz), f32),
        in_specs=[
            pl.BlockSpec(memory_space=pl.ANY),
            pl.BlockSpec(memory_space=pltpu.VMEM),
            pl.BlockSpec(memory_space=pltpu.VMEM),
        ],
        out_specs=pl.BlockSpec(memory_space=pl.ANY),
        scratch_shapes=scratch,
        compiler_params=pltpu.CompilerParams(
            collective_id=0, has_side_effects=True, vmem_limit_bytes=VMEM_MIB * 1024 * 1024
        ),
    )(data_slab, first_factor.T, second_factor.T)


def solution(mesh):
    nz, nc = mesh.shape["fib"], mesh.shape["col"]

    def on_each(data_slab, first_factor, second_factor):
        cells = data_slab.shape[2]
        if nc == 4 and nz == 4 and cells == nz * nc * LANES:
            return fused(nz, data_slab, first_factor, second_factor)
        return on_device(data_slab, first_factor, second_factor)

    in_specs = (P(("groups", "fib"), "col", None), P(), P())
    out_specs = P(("groups", "col"), None, "fib")
    return jax.shard_map(
        on_each, mesh=mesh, in_specs=in_specs, out_specs=out_specs, check_vma=False
    )
```
